1024 devices in a mesh: row: 64 (over x, z_hi, y), col: 16 (over z_lo, core).
Axes of the slice: x: 4, y: 4, z: 32 (z_hi: 4, z_lo: 8; z = z_hi * 8 + z_lo), core: 2. Of those that a mesh axis runs over, the one named last changes fastest.
Arguments:
- a_panels: bfloat16 [64, 16, 4, 128, 128], P('row', 'col'), may hold values from -0.5 to 0.5
- b_panels: bfloat16 [64, 16, 4, 128, 128], P('row', 'col'), may hold values from -6 to 6
- pair_lists: int32 [64, 16, 4, 3, 16], P('row', 'col'), may hold values from 0 to 31, as said below
- pair_counts: int32 [64, 16, 4], P('row', 'col'), may hold values from 1 to 16
- keep_mask: int32 [64, 16, 32], P('row', 'col'), may hold values 0 or 1
- send_order: int32 [64, 16, 32], P('row', 'col'), may hold values from 0 to 31, each once within a row
- recv_order: int32 [64, 16, 32], P('row', 'col'), may hold values from 0 to 31, each once within a row
Outputs:
- returned: bfloat16 [64, 16, 32, 128, 128], P('row', 'col')
The draws below stay inside these ranges and needn't reach their ends.
Inputs may be any that keep to these rules, and one draw needn't show every extreme that they name: pair_lists[..., 0, :] is below 4, pair_lists[..., 1, :] below 4, pair_lists[..., 2, :] below 32; entries at or after pair_counts are not used.
All inputs are finite; a program needn't handle non-finite values. No bound on the sum of `keep_mask` on one device may be relied on, other than what follows from the above.
Results may differ from the reference program's by a relative error of at most 0.001.
Values may be sent and summed in bfloat16 or wider, within the bound.
No kernel may reach another device: no remote copies, remote signals or barrier semaphores. Data moves between devices by JAX's collectives and lax.ppermute only.
A program may use at most 32 MiB of HBM per device.

```python
from functools import partial
import jax
import jax.numpy as jnp
from jax import lax

BS = 128
SA = 4
SB = 4
PP = 16
STEPS = 4
RC = 2
CS = 32
N_ROW = 64
N_COL = 16


def draw_pair_lists(key, part):
    key = jax.random.fold_in(key, 11)
    first_key, second_key, third_key = jax.random.split(key, 3)
    shape = (N_ROW, N_COL, STEPS, PP)
    left_index = jax.random.randint(first_key, shape, 0, SA)
    right_index = jax.random.randint(second_key, shape, 0, SB)
    target_index = jax.random.randint(third_key, shape, 0, CS)
    return jnp.stack([left_index, right_index, target_index], axis=3).astype(jnp.int32)


def draw_pair_counts(key, part):
    key = jax.random.fold_in(key, 12)
    flag_key, high_key, low_key, spot_key = jax.random.split(key, 4)
    shape = (N_ROW, N_COL, STEPS)
    heavy = jax.random.randint(flag_key, (N_ROW, N_COL, 1), 0, 4) == 0
    high_counts = jax.random.randint(high_key, shape, PP // 2, PP + 1)
    low_counts = jax.random.randint(low_key, shape, 1, PP // 2 + 1)
    counts = jnp.where(heavy, high_counts, low_counts).reshape(-1)
    spot = jax.random.randint(spot_key, (), 0, N_ROW * N_COL * STEPS)
    counts = jnp.where(jnp.arange(N_ROW * N_COL * STEPS) == spot, PP, counts)
    return counts.reshape(shape).astype(jnp.int32)


def place_ends(drawn, own_key, low, largest):
    longest = drawn.shape.index(max(drawn.shape))
    spots = []
    for shift in (0, 1):
        where = [jax.random.randint(jax.random.fold_in(own_key, axis), (), 0, length) for axis, length in enumerate(drawn.shape)]
        where[longest] = (where[longest] + shift) % drawn.shape[longest]
        spots.append(tuple(where))
    return drawn.at[spots[0]].set(low).at[spots[1]].set(largest)


def level_of(own_key, extent, cuts, low, high):
    level = 1.0
    for axis_at, blocks in cuts:
        heights = jax.random.uniform(jax.random.fold_in(jax.random.fold_in(own_key, 6), axis_at), (blocks,), jnp.float32, low / len(cuts), high / len(cuts))
        level = level * jnp.repeat(jnp.exp(heights), extent[axis_at] // blocks).reshape((-1,) + (1,) * (len(extent) - 1 - axis_at))
    return level


def normal_values(rng, shape, spread, limit, cuts=(), kind=jnp.bfloat16):
    values = jax.random.normal(rng, shape, jnp.float32) * spread
    if len(cuts) > 0:
        values = level_of(rng, shape, cuts, -0.22, 0.18) * values
    return jnp.clip(values, min=-limit, max=limit).astype(kind)


def setup_inputs(seed: int = 0) -> dict:
    key_of = jax.random.split(jax.random.key(seed), 8)
    return {
        "a_panels": normal_values(key_of[0], (N_ROW, N_COL, SA, BS, BS), (BS * STEPS * PP // (2 * N_COL * RC)) ** -0.5, 0.5, ((0, 64), (1, 16))),
        "b_panels": normal_values(key_of[1], (N_ROW, N_COL, SB, BS, BS), 1.0, 6.0, ((0, 64), (1, 16))),
        "pair_lists": draw_pair_lists(jax.random.fold_in(key_of[7], 71), 0),
        "pair_counts": draw_pair_counts(jax.random.fold_in(key_of[7], 71), 0),
        "keep_mask": place_ends((jax.random.randint(key_of[4], (N_ROW, N_COL, CS), 0, 4) < 3).astype(jnp.int32), jax.random.fold_in(key_of[4], 1), 0, 1),
        "send_order": jax.vmap(lambda own: jax.random.permutation(own, CS))(jax.random.split(key_of[5], N_ROW * N_COL)).reshape((N_ROW, N_COL, CS)).astype(jnp.int32),
        "recv_order": jax.vmap(lambda own: jax.random.permutation(own, CS))(jax.random.split(key_of[6], N_ROW * N_COL)).reshape((N_ROW, N_COL, CS)).astype(jnp.int32),
    }


def pick_blocks(blocks, indices):
    return blocks[indices]


def row_products(row_index, a_panels, b_panels, pair_lists, pair_counts, keep_mask, send_order):
    total = jnp.zeros((N_COL, CS, BS, BS), jnp.float32)
    a_row = lax.dynamic_index_in_dim(a_panels, row_index, 0, keepdims=False)
    pairs_row = lax.dynamic_index_in_dim(pair_lists, row_index, 0, keepdims=False)
    counts_row = lax.dynamic_index_in_dim(pair_counts, row_index, 0, keepdims=False)
    keep_row = lax.dynamic_index_in_dim(keep_mask, row_index, 0, keepdims=False)
    send_row = lax.dynamic_index_in_dim(send_order, row_index, 0, keepdims=False)
    positions = jnp.arange(PP, dtype=jnp.int32)
    for turn_index in range(STEPS):
        a_turn = jnp.roll(a_row, -turn_index, axis=0)
        b_turn = lax.dynamic_index_in_dim(b_panels, ((row_index + turn_index) % N_ROW).astype(jnp.int32), 0, keepdims=False)
        left_blocks = jax.vmap(pick_blocks)(a_turn, pairs_row[:, turn_index, 0, :]).astype(jnp.float32)
        right_blocks = jax.vmap(pick_blocks)(b_turn, pairs_row[:, turn_index, 1, :]).astype(jnp.float32)
        products = jnp.einsum('cpij,cpjk->cpik', left_blocks, right_blocks)
        live = (positions[None, :] < counts_row[:, turn_index][:, None]).astype(jnp.float32)
        products = products * live[:, :, None, None]
        total = total + jax.vmap(partial(jax.ops.segment_sum, num_segments=CS))(products, pairs_row[:, turn_index, 2, :])
    filtered = (total * keep_row[:, :, None, None].astype(jnp.float32)).astype(jnp.bfloat16)
    ordered = jax.vmap(pick_blocks)(filtered, send_row)
    return ordered.reshape(N_COL, N_COL, RC, BS, BS)


def reference(a_panels, b_panels, pair_lists, pair_counts, keep_mask, send_order, recv_order):
    def one_row(row_index):
        return row_products(row_index, a_panels, b_panels, pair_lists, pair_counts, keep_mask, send_order)

    ordered = lax.map(one_row, jnp.arange(N_ROW, dtype=jnp.int32))
    received = jnp.swapaxes(ordered, 1, 2).reshape(N_ROW, N_COL, CS, BS, BS)
    return jax.vmap(jax.vmap(pick_blocks))(received, recv_order)
```

```python
import jax
import jax.numpy as jnp
from jax import lax
from jax.experimental import pallas as pl
from jax.experimental.pallas import tpu as pltpu
from jax.sharding import PartitionSpec as P

RUN = 4


def shift(x, axis, by):
    peers = lax.axis_size(axis)
    return lax.ppermute(x, axis, [((i + by) % peers, i) for i in range(peers)])


def row_hop(x, by, targets):
    rows = lax.axis_size("row")
    return lax.ppermute(
        x, "row", [((i + by) % rows, i) for i in range(rows) if i % RUN in targets]
    )


def multiply_kernel(
    place, counts, pairs, keep, order,
    a0, a1, a2, a3, b0, b1_near, b1_far, b2_near, b2_far, b3,
    out, prod, acc,
):
    blocks, size, _ = a0.shape
    acc[...] = jnp.zeros_like(acc)

    def form(turn, left, right):
        rows = left[...].reshape(blocks * size, size)
        for b in range(0, blocks, 2):
            wide = jnp.concatenate([right[b], right[b + 1]], axis=1)
            result = jnp.dot(rows, wide, preferred_element_type=jnp.float32)
            for a in range(blocks):
                for half in range(2):
                    prod[turn, a * blocks + b + half] = result[
                        a * size : (a + 1) * size, half * size : (half + 1) * size
                    ]

    def add(turn):
        def one(p, carry):
            slot = pairs[turn, 2, p]
            which = pairs[turn, 0, p] * blocks + pairs[turn, 1, p]
            acc[slot] += prod[turn, which]
            return carry

        lax.fori_loop(0, counts[turn], one, 0)

    def choose(turn, left, near, far, bound):
        @pl.when(place[0] < bound)
        def _():
            form(turn, left, near)

        @pl.when(place[0] >= bound)
        def _():
            form(turn, left, far)

    form(0, a0, b0)
    choose(1, a1, b1_near, b1_far, 3)
    choose(2, a2, b2_near, b2_far, 2)
    form(3, a3, b3)
    for turn in range(4):
        add(turn)

    def hand(o, carry):
        slot = order[o]
        kept = keep[slot].astype(jnp.float32)
        out[o] = (acc[slot] * kept).astype(out.dtype)
        return carry

    lax.fori_loop(0, out.shape[0], hand, 0)


def multiply(place, counts, pairs, keep, order, panels, slots):
    blocks, size, _ = panels[0].shape
    turns = pairs.shape[0]
    smem = pl.BlockSpec(memory_space=pltpu.SMEM)
    vmem = pl.BlockSpec(memory_space=pltpu.VMEM)
    return pl.pallas_call(
        multiply_kernel,
        out_shape=jax.ShapeDtypeStruct((slots, size, size), panels[0].dtype),
        in_specs=[smem] * 5 + [vmem] * len(panels),
        out_specs=vmem,
        scratch_shapes=[
            pltpu.VMEM((turns, blocks * blocks, size, size), jnp.float32),
            pltpu.VMEM((slots, size, size), jnp.float32),
        ],
        compiler_params=pltpu.CompilerParams(vmem_limit_bytes=24 << 20),
        name="multiply",
    )(place, counts, pairs, keep, order, *panels)


def body(a_panels, b_panels, pair_lists, pair_counts, keep_mask, send_order, recv_order):
    a0 = a_panels[0, 0]
    b0 = b_panels[0, 0]
    b3 = shift(b0, "row", 3)
    b1_near = row_hop(b0, 1, (0, 1, 2))
    b2_near = row_hop(b0, 2, (0, 1))
    a1, a2, a3 = (shift(a0, "col", by) for by in (1, 2, 3))
    b2_far = row_hop(b3, -1, (2, 3))
    b1_far = row_hop(b3, -2, (3,))
    place = lax.rem(lax.axis_index("row"), RUN).astype(jnp.int32).reshape(1)
    ordered = multiply(
        place, pair_counts[0, 0], pair_lists[0, 0], keep_mask[0, 0], send_order[0, 0],
        (a0, a1, a2, a3, b0, b1_near, b1_far, b2_near, b2_far, b3), keep_mask.shape[2],
    )
    received = lax.all_to_all(ordered, "col", split_axis=0, concat_axis=0, tiled=True)
    return received[recv_order[0, 0]][None, None]


def solution(mesh):
    return jax.shard_map(
        body,
        mesh=mesh,
        in_specs=(
            P("row", "col", None, None, None),
            P("row", "col", None, None, None),
            P("row", "col", None, None, None),
            P("row", "col", None),
            P("row", "col", None),
            P("row", "col", None),
            P("row", "col", None),
        ),
        out_specs=P("row", "col", None, None, None),
        check_vma=False,
    )
```

```python
import jax
import jax.numpy as jnp
from jax import lax
from jax.experimental import pallas as pl
from jax.experimental.pallas import tpu as pltpu
from jax.sharding import PartitionSpec as P

RUN = 4


def shift(x, axis, by):
    peers = lax.axis_size(axis)
    return lax.ppermute(x, axis, [((i + by) % peers, i) for i in range(peers)])


def row_hop(x, by, targets):
    rows = lax.axis_size("row")
    return lax.ppermute(
        x, "row", [((i + by) % rows, i) for i in range(rows) if i % RUN in targets]
    )


def form(left, right, prod):
    blocks, size, _ = left.shape
    rows = left[...].reshape(blocks * size, size)
    for b in range(0, blocks, 2):
        wide = jnp.concatenate([right[b], right[b + 1]], axis=1)
        result = jnp.dot(rows, wide, preferred_element_type=jnp.float32)
        for a in range(blocks):
            for half in range(2):
                prod[a * blocks + b + half] = result[
                    a * size : (a + 1) * size, half * size : (half + 1) * size
                ]


def add(acc, prod, pairs, count, turn, blocks):
    def one(p, carry):
        which = pairs[turn, 0, p] * blocks + pairs[turn, 1, p]
        acc[pairs[turn, 2, p]] += prod[which]
        return carry

    lax.fori_loop(0, count, one, 0)


def first_kernel(counts, pairs, a0, b0, acc, prod):
    form(a0, b0, prod)
    acc[...] = jnp.zeros_like(acc)
    add(acc, prod, pairs, counts[0], 0, a0.shape[0])


def middle_kernel(
    place, counts, pairs, begun, a1, a2, a3, near1, near2, cross, acc, prod,
):
    blocks = a1.shape[0]
    form(a3, cross, prod)
    acc[...] = begun[...]
    add(acc, prod, pairs, counts[3], 3, blocks)

    @pl.when(place[0] < 3)
    def _():
        form(a1, near1, prod)
        add(acc, prod, pairs, counts[1], 1, blocks)

    @pl.when(place[0] < 2)
    def _():
        form(a2, near2, prod)
        add(acc, prod, pairs, counts[2], 2, blocks)


def last_kernel(
    place, counts, pairs, keep, order, nearly, a1, a2, far1, far2, out, prod, acc,
):
    blocks = a1.shape[0]
    acc[...] = nearly[...]

    @pl.when(place[0] >= 2)
    def _():
        form(a2, far2, prod)
        add(acc, prod, pairs, counts[2], 2, blocks)

    @pl.when(place[0] >= 3)
    def _():
        form(a1, far1, prod)
        add(acc, prod, pairs, counts[1], 1, blocks)

    def hand(o, carry):
        slot = order[o]
        kept = keep[slot].astype(jnp.float32)
        out[o] = (acc[slot] * kept).astype(out.dtype)
        return carry

    lax.fori_loop(0, out.shape[0], hand, 0)


SMEM = pl.BlockSpec(memory_space=pltpu.SMEM)
VMEM = pl.BlockSpec(memory_space=pltpu.VMEM)


def begin(counts, pairs, a0, b0, slots):
    blocks, size, _ = a0.shape
    return pl.pallas_call(
        first_kernel,
        out_shape=jax.ShapeDtypeStruct((slots, size, size), jnp.float32),
        in_specs=[SMEM] * 2 + [VMEM] * 2,
        out_specs=VMEM,
        scratch_shapes=[pltpu.VMEM((blocks * blocks, size, size), jnp.float32)],
        compiler_params=pltpu.CompilerParams(vmem_limit_bytes=16 << 20),
        name="begin",
    )(counts, pairs, a0, b0)


def middle(place, counts, pairs, begun, panels):
    blocks, size, _ = panels[0].shape
    return pl.pallas_call(
        middle_kernel,
        out_shape=jax.ShapeDtypeStruct(begun.shape, begun.dtype),
        in_specs=[SMEM] * 3 + [VMEM] * (1 + len(panels)),
        out_specs=VMEM,
        scratch_shapes=[
            pltpu.VMEM((blocks * blocks, size, size), jnp.float32),
        ],
        compiler_params=pltpu.CompilerParams(vmem_limit_bytes=20 << 20),
        name="middle",
    )(place, counts, pairs, begun, *panels)


def finish(place, counts, pairs, keep, order, nearly, panels):
    blocks, size, _ = panels[0].shape
    slots = keep.shape[0]
    return pl.pallas_call(
        last_kernel,
        out_shape=jax.ShapeDtypeStruct((slots, size, size), panels[0].dtype),
        in_specs=[SMEM] * 5 + [VMEM] * (1 + len(panels)),
        out_specs=VMEM,
        scratch_shapes=[
            pltpu.VMEM((blocks * blocks, size, size), jnp.float32),
            pltpu.VMEM((slots, size, size), jnp.float32),
        ],
        compiler_params=pltpu.CompilerParams(vmem_limit_bytes=20 << 20),
        name="finish",
    )(place, counts, pairs, keep, order, nearly, *panels)


def body(a_panels, b_panels, pair_lists, pair_counts, keep_mask, send_order, recv_order):
    a0 = a_panels[0, 0]
    b0 = b_panels[0, 0]
    pairs, counts = pair_lists[0, 0], pair_counts[0, 0]
    keep, order = keep_mask[0, 0], send_order[0, 0]
    row = lax.axis_index("row").astype(jnp.int32)
    begun = begin(counts, pairs, a0, b0, keep.shape[0])
    cross = shift(b0, "row", 3)
    near1 = row_hop(b0, 1, (0, 1, 2))
    near2 = row_hop(b0, 2, (0, 1))
    a1, a2 = (shift(a0, "col", by) for by in (1, 2))
    held, near1, begun = lax.optimization_barrier((a0, near1, begun))
    a3 = shift(held, "col", 3)
    cross, near2 = lax.optimization_barrier((cross, near2))
    far1 = row_hop(cross, -2, (3,))
    far2 = row_hop(cross, -1, (2, 3))
    place = lax.rem(row, RUN).reshape(1)
    nearly = middle(
        place, counts, pairs, begun, (a1, a2, a3, near1, near2, cross)
    )
    ordered = finish(place, counts, pairs, keep, order, nearly, (a1, a2, far1, far2))
    received = lax.all_to_all(ordered, "col", split_axis=0, concat_axis=0, tiled=True)
    return received[recv_order[0, 0]][None, None]


def solution(mesh):
    return jax.shard_map(
        body,
        mesh=mesh,
        in_specs=(
            P("row", "col", None, None, None),
            P("row", "col", None, None, None),
            P("row", "col", None, None, None),
            P("row", "col", None),
            P("row", "col", None),
            P("row", "col", None),
            P("row", "col", None),
        ),
        out_specs=P("row", "col", None, None, None),
        check_vma=False,
    )
```

```python
import jax
import jax.numpy as jnp
from jax import lax
from jax.experimental import pallas as pl
from jax.experimental.pallas import tpu as pltpu
from jax.sharding import PartitionSpec as P

RUN = 4


def shift(x, axis, by):
    peers = lax.axis_size(axis)
    return lax.ppermute(x, axis, [((i + by) % peers, i) for i in range(peers)])


def row_hop(x, by, targets):
    rows = lax.axis_size("row")
    return lax.ppermute(
        x, "row", [((i + by) % rows, i) for i in range(rows) if i % RUN in targets]
    )


def form(left, right, prod):
    blocks, size, _ = left.shape
    rows = left[...].reshape(blocks * size, size)
    for b in range(0, blocks, 2):
        wide = jnp.concatenate([right[b], right[b + 1]], axis=1)
        result = jnp.dot(rows, wide, preferred_element_type=jnp.float32)
        for a in range(blocks):
            for half in range(2):
                prod[a * blocks + b + half] = result[
                    a * size : (a + 1) * size, half * size : (half + 1) * size
                ]


TURNS, PAIRS, SLOTS = 4, 16, 32
COUNTS = 1
LISTS = COUNTS + TURNS
MASK = LISTS + TURNS * 3 * PAIRS
ORDER = MASK + SLOTS


def add(acc, prod, ints, turn, blocks):
    base = LISTS + turn * 3 * PAIRS

    def one(p, carry):
        which = ints[base + p] * blocks + ints[base + PAIRS + p]
        acc[ints[base + 2 * PAIRS + p]] += prod[which]
        return carry

    lax.fori_loop(0, ints[COUNTS + turn], one, 0)


def first_kernel(ints, a0, b0, acc, prod):
    form(a0, b0, prod)
    acc[...] = jnp.zeros_like(acc)
    add(acc, prod, ints, 0, a0.shape[0])


def middle_kernel(ints, begun, a1, a2, a3, near1, near2, cross, acc, prod):
    del begun
    blocks, spot = a1.shape[0], ints[0]
    form(a3, cross, prod)
    add(acc, prod, ints, 3, blocks)

    @pl.when(spot < RUN - 1)
    def _():
        form(a1, near1, prod)
        add(acc, prod, ints, 1, blocks)

    @pl.when(spot < RUN - 2)
    def _():
        form(a2, near2, prod)
        add(acc, prod, ints, 2, blocks)


def last_kernel(ints, nearly, a1, a2, far1, far2, out, acc, prod, ready, sems):
    del nearly
    blocks, spot = a1.shape[0], ints[0]

    @pl.when(spot >= RUN - 2)
    def _():
        form(a2, far2, prod)
        add(acc, prod, ints, 2, blocks)

    @pl.when(spot == RUN - 1)
    def _():
        form(a1, far1, prod)
        add(acc, prod, ints, 1, blocks)

    copies = []
    for o in range(SLOTS):
        slot = ints[ORDER + o]
        kept = ints[MASK + slot].astype(jnp.float32)
        ready[o] = (acc[slot] * kept).astype(ready.dtype)
        if o % 4 == 3:
            part = pl.ds(o - 3, 4)
            copies.append(pltpu.make_async_copy(ready.at[part], out.at[part], sems.at[o // 4]))
            copies[-1].start()
    for copy in copies:
        copy.wait()


SMEM = pl.BlockSpec(memory_space=pltpu.SMEM)
VMEM = pl.BlockSpec(memory_space=pltpu.VMEM)
FAR = pl.BlockSpec(memory_space=pl.ANY)


def begin(ints, a0, b0):
    blocks, size, _ = a0.shape
    return pl.pallas_call(
        first_kernel,
        out_shape=jax.ShapeDtypeStruct((SLOTS, size, size), jnp.float32),
        in_specs=[SMEM, VMEM, VMEM],
        out_specs=VMEM,
        scratch_shapes=[pltpu.VMEM((blocks * blocks, size, size), jnp.float32)],
        compiler_params=pltpu.CompilerParams(vmem_limit_bytes=16 << 20),
        name="begin",
    )(ints, a0, b0)


def middle(ints, begun, panels):
    blocks, size, _ = panels[0].shape
    return pl.pallas_call(
        middle_kernel,
        out_shape=jax.ShapeDtypeStruct(begun.shape, begun.dtype),
        in_specs=[SMEM] + [VMEM] * (1 + len(panels)),
        out_specs=VMEM,
        scratch_shapes=[pltpu.VMEM((blocks * blocks, size, size), jnp.float32)],
        input_output_aliases={1: 0},
        compiler_params=pltpu.CompilerParams(vmem_limit_bytes=20 << 20),
        name="middle",
    )(ints, begun, *panels)


def finish(ints, nearly, panels):
    blocks, size, _ = panels[0].shape
    ordered = jax.ShapeDtypeStruct(nearly.shape, panels[0].dtype)
    return pl.pallas_call(
        last_kernel,
        out_shape=[ordered, jax.ShapeDtypeStruct(nearly.shape, nearly.dtype)],
        in_specs=[SMEM] + [VMEM] * (1 + len(panels)),
        out_specs=[FAR, VMEM],
        scratch_shapes=[
            pltpu.VMEM((blocks * blocks, size, size), jnp.float32),
            pltpu.VMEM(ordered.shape, ordered.dtype),
            pltpu.SemaphoreType.DMA((SLOTS // 4,)),
        ],
        input_output_aliases={1: 1},
        compiler_params=pltpu.CompilerParams(vmem_limit_bytes=20 << 20),
        name="finish",
    )(ints, nearly, *panels)[0]


def body(a_panels, b_panels, pair_lists, pair_counts, keep_mask, send_order, recv_order):
    a0 = a_panels[0, 0]
    b0 = b_panels[0, 0]
    row = lax.axis_index("row").astype(jnp.int32)
    ints = jnp.concatenate([
        lax.rem(row, RUN).reshape(1), pair_counts.reshape(-1), pair_lists.reshape(-1),
        keep_mask.reshape(-1), send_order.reshape(-1),
    ])
    begun = begin(ints, a0, b0)
    cross = shift(b0, "row", 3)
    near1 = row_hop(b0, 1, (0, 1, 2))
    a1, a2, a3 = (shift(a0, "col", by) for by in (1, 2, 3))
    near2 = row_hop(near1, 1, (0, 1))
    cross, near2, begun = lax.optimization_barrier((cross, near2, begun))
    far2 = row_hop(cross, -1, (2, 3))
    far1 = row_hop(cross, -2, (3,))
    nearly = middle(ints, begun, (a1, a2, a3, near1, near2, cross))
    ordered = finish(ints, nearly, (a1, a2, far1, far2))
    received = lax.all_to_all(ordered, "col", split_axis=0, concat_axis=0, tiled=True)
    return received[recv_order[0, 0]][None, None]


def solution(mesh):
    return jax.shard_map(
        body,
        mesh=mesh,
        in_specs=(
            P("row", "col", None, None, None),
            P("row", "col", None, None, None),
            P("row", "col", None, None, None),
            P("row", "col", None),
            P("row", "col", None),
            P("row", "col", None),
            P("row", "col", None),
        ),
        out_specs=P("row", "col", None, None, None),
        check_vma=False,
    )
```

```python
import jax
import jax.numpy as jnp
from jax import lax
from jax.experimental import pallas as pl
from jax.experimental.pallas import tpu as pltpu
from jax.sharding import PartitionSpec as P

RUN = 4


def shift(x, axis, by):
    peers = lax.axis_size(axis)
    return lax.ppermute(x, axis, [((i + by) % peers, i) for i in range(peers)])


def row_hop(x, by, targets):
    rows = lax.axis_size("row")
    return lax.ppermute(
        x, "row", [((i + by) % rows, i) for i in range(rows) if i % RUN in targets]
    )


def form(left, right, prod):
    blocks, size, _ = left.shape
    rows = left[...].reshape(blocks * size, size)
    for b in range(0, blocks, 2):
        wide = jnp.concatenate([right[b], right[b + 1]], axis=1)
        result = jnp.dot(rows, wide, preferred_element_type=jnp.float32)
        for a in range(blocks):
            for half in range(2):
                prod[a * blocks + b + half] = result[
                    a * size : (a + 1) * size, half * size : (half + 1) * size
                ]


TURNS, PAIRS, SLOTS = 4, 16, 32
COUNTS = 1
LISTS = COUNTS + TURNS
MASK = LISTS + TURNS * 3 * PAIRS
ORDER = MASK + SLOTS


def add(acc, prod, ints, turn, blocks):
    base = LISTS + turn * 3 * PAIRS

    def one(p, carry):
        which = ints[base + p] * blocks + ints[base + PAIRS + p]
        acc[ints[base + 2 * PAIRS + p]] += prod[which]
        return carry

    lax.fori_loop(0, ints[COUNTS + turn], one, 0)


def first_kernel(ints, a0, b0, acc, prod):
    form(a0, b0, prod)
    acc[...] = jnp.zeros_like(acc)
    add(acc, prod, ints, 0, a0.shape[0])


def middle_kernel(ints, begun, a1, a2, a3, near1, fellow, cross, acc, prod):
    del begun
    blocks, spot = a1.shape[0], ints[0]
    form(a3, cross, prod)
    add(acc, prod, ints, 3, blocks)

    @pl.when(spot < RUN - 1)
    def _():
        form(a1, near1, prod)
        add(acc, prod, ints, 1, blocks)

    @pl.when(spot < RUN - 2)
    def _():
        form(a2, fellow.at[1], prod)
        add(acc, prod, ints, 2, blocks)


def last_kernel(ints, nearly, a1, a2, far1, far2, out, acc, prod, ready, sems):
    del nearly
    blocks, spot = a1.shape[0], ints[0]

    @pl.when(spot >= RUN - 2)
    def _():
        form(a2, far2, prod)
        add(acc, prod, ints, 2, blocks)

    @pl.when(spot == RUN - 1)
    def _():
        form(a1, far1, prod)
        add(acc, prod, ints, 1, blocks)

    copies = []
    for o in range(SLOTS):
        slot = ints[ORDER + o]
        kept = ints[MASK + slot].astype(jnp.float32)
        ready[o] = (acc[slot] * kept).astype(ready.dtype)
        if o % 4 == 3:
            part = pl.ds(o - 3, 4)
            copies.append(pltpu.make_async_copy(ready.at[part], out.at[part], sems.at[o // 4]))
            copies[-1].start()
    for copy in copies:
        copy.wait()


SMEM = pl.BlockSpec(memory_space=pltpu.SMEM)
VMEM = pl.BlockSpec(memory_space=pltpu.VMEM)
FAR = pl.BlockSpec(memory_space=pl.ANY)


def begin(ints, a0, b0):
    blocks, size, _ = a0.shape
    return pl.pallas_call(
        first_kernel,
        out_shape=jax.ShapeDtypeStruct((SLOTS, size, size), jnp.float32),
        in_specs=[SMEM, VMEM, VMEM],
        out_specs=VMEM,
        scratch_shapes=[pltpu.VMEM((blocks * blocks, size, size), jnp.float32)],
        compiler_params=pltpu.CompilerParams(vmem_limit_bytes=16 << 20),
        name="begin",
    )(ints, a0, b0)


def middle(ints, begun, panels):
    blocks, size, _ = panels[0].shape
    return pl.pallas_call(
        middle_kernel,
        out_shape=jax.ShapeDtypeStruct(begun.shape, begun.dtype),
        in_specs=[SMEM] + [VMEM] * (1 + len(panels)),
        out_specs=VMEM,
        scratch_shapes=[pltpu.VMEM((blocks * blocks, size, size), jnp.float32)],
        input_output_aliases={1: 0},
        compiler_params=pltpu.CompilerParams(vmem_limit_bytes=20 << 20),
        name="middle",
    )(ints, begun, *panels)


def finish(ints, nearly, panels):
    blocks, size, _ = panels[0].shape
    ordered = jax.ShapeDtypeStruct(nearly.shape, panels[0].dtype)
    return pl.pallas_call(
        last_kernel,
        out_shape=[ordered, jax.ShapeDtypeStruct(nearly.shape, nearly.dtype)],
        in_specs=[SMEM] + [VMEM] * (1 + len(panels)),
        out_specs=[FAR, VMEM],
        scratch_shapes=[
            pltpu.VMEM((blocks * blocks, size, size), jnp.float32),
            pltpu.VMEM(ordered.shape, ordered.dtype),
            pltpu.SemaphoreType.DMA((SLOTS // 4,)),
        ],
        input_output_aliases={1: 1},
        compiler_params=pltpu.CompilerParams(vmem_limit_bytes=20 << 20),
        name="finish",
    )(ints, nearly, *panels)[0]


def body(a_panels, b_panels, pair_lists, pair_counts, keep_mask, send_order, recv_order):
    a0 = a_panels[0, 0]
    b0 = b_panels[0, 0]
    row = lax.axis_index("row").astype(jnp.int32)
    ints = jnp.concatenate([
        lax.rem(row, RUN).reshape(1), pair_counts.reshape(-1), pair_lists.reshape(-1),
        keep_mask.reshape(-1), send_order.reshape(-1),
    ])
    cross = shift(b0, "row", 3)
    near1 = row_hop(b0, 1, (0, 1, 2))
    a1, a2, a3 = (shift(a0, "col", by) for by in (1, 2, 3))
    rows = lax.axis_size("row")
    fellow = lax.all_gather(
        b0, "row", axis_index_groups=[[i, i + 2] for i in range(rows) if i % RUN < 2]
    )
    cross, near1, fellow, ints = lax.optimization_barrier((cross, near1, fellow, ints))
    far2 = row_hop(cross, -1, (2, 3))
    far1 = row_hop(cross, -2, (3,))
    begun = begin(ints, a0, b0)
    nearly = middle(ints, begun, (a1, a2, a3, near1, fellow, cross))
    ordered = finish(ints, nearly, (a1, a2, far1, far2))
    received = lax.all_to_all(ordered, "col", split_axis=0, concat_axis=0, tiled=True)
    return received[recv_order[0, 0]][None, None]


def solution(mesh):
    return jax.shard_map(
        body,
        mesh=mesh,
        in_specs=(
            P("row", "col", None, None, None),
            P("row", "col", None, None, None),
            P("row", "col", None, None, None),
            P("row", "col", None),
            P("row", "col", None),
            P("row", "col", None),
            P("row", "col", None),
        ),
        out_specs=P("row", "col", None, None, None),
        check_vma=False,
    )
```

```python
import jax
import jax.numpy as jnp
from jax import lax
from jax.experimental import pallas as pl
from jax.experimental.pallas import tpu as pltpu
from jax.sharding import PartitionSpec as P

RUN = 4


def shift(x, axis, by):
    peers = lax.axis_size(axis)
    return lax.ppermute(x, axis, [((i + by) % peers, i) for i in range(peers)])


def row_hop(x, by, targets):
    rows = lax.axis_size("row")
    return lax.ppermute(
        x, "row", [((i + by) % rows, i) for i in range(rows) if i % RUN in targets]
    )


def form(left, right, prod):
    blocks, size, _ = left.shape
    rows = left[...].reshape(blocks * size, size)
    for b in range(0, blocks, 2):
        wide = jnp.concatenate([right[b], right[b + 1]], axis=1)
        result = jnp.dot(rows, wide, preferred_element_type=jnp.float32)
        for a in range(blocks):
            for half in range(2):
                prod[a * blocks + b + half] = result[
                    a * size : (a + 1) * size, half * size : (half + 1) * size
                ]


TURNS, PAIRS, SLOTS = 4, 16, 32
COUNTS = 1
LISTS = COUNTS + TURNS
MASK = LISTS + TURNS * 3 * PAIRS
ORDER = MASK + SLOTS


def add(acc, prod, ints, turn, blocks):
    base = LISTS + turn * 3 * PAIRS

    def one(p, carry):
        which = ints[base + p] * blocks + ints[base + PAIRS + p]
        acc[ints[base + 2 * PAIRS + p]] += prod[which]
        return carry

    lax.fori_loop(0, ints[COUNTS + turn], one, 0)


def first_kernel(ints, a0, fellow, acc, prod):
    form(a0, fellow.at[lax.div(ints[0], 2)], prod)
    acc[...] = jnp.zeros_like(acc)
    add(acc, prod, ints, 0, a0.shape[0])


def middle_kernel(ints, begun, a1, a2, a3, near1, fellow, cross, acc, prod):
    del begun
    blocks, spot = a1.shape[0], ints[0]
    form(a3, cross, prod)
    add(acc, prod, ints, 3, blocks)

    @pl.when(spot < RUN - 1)
    def _():
        form(a1, near1, prod)
        add(acc, prod, ints, 1, blocks)

    @pl.when(spot < RUN - 2)
    def _():
        form(a2, fellow.at[1], prod)
        add(acc, prod, ints, 2, blocks)


def last_kernel(ints, nearly, a1, a2, far1, far2, out, acc, prod, ready, sems):
    del nearly
    blocks, spot = a1.shape[0], ints[0]

    @pl.when(spot >= RUN - 2)
    def _():
        form(a2, far2, prod)
        add(acc, prod, ints, 2, blocks)

    @pl.when(spot == RUN - 1)
    def _():
        form(a1, far1, prod)
        add(acc, prod, ints, 1, blocks)

    copies = []
    for o in range(SLOTS):
        slot = ints[ORDER + o]
        kept = ints[MASK + slot].astype(jnp.float32)
        ready[o] = (acc[slot] * kept).astype(ready.dtype)
        if o % 4 == 3:
            part = pl.ds(o - 3, 4)
            copies.append(pltpu.make_async_copy(ready.at[part], out.at[part], sems.at[o // 4]))
            copies[-1].start()
    for copy in copies:
        copy.wait()


SMEM = pl.BlockSpec(memory_space=pltpu.SMEM)
VMEM = pl.BlockSpec(memory_space=pltpu.VMEM)
FAR = pl.BlockSpec(memory_space=pl.ANY)


def begin(ints, a0, fellow):
    blocks, size, _ = a0.shape
    return pl.pallas_call(
        first_kernel,
        out_shape=jax.ShapeDtypeStruct((SLOTS, size, size), jnp.float32),
        in_specs=[SMEM, VMEM, VMEM],
        out_specs=VMEM,
        scratch_shapes=[pltpu.VMEM((blocks * blocks, size, size), jnp.float32)],
        compiler_params=pltpu.CompilerParams(vmem_limit_bytes=16 << 20),
        name="begin",
    )(ints, a0, fellow)


def middle(ints, begun, panels):
    blocks, size, _ = panels[0].shape
    return pl.pallas_call(
        middle_kernel,
        out_shape=jax.ShapeDtypeStruct(begun.shape, begun.dtype),
        in_specs=[SMEM] + [VMEM] * (1 + len(panels)),
        out_specs=VMEM,
        scratch_shapes=[pltpu.VMEM((blocks * blocks, size, size), jnp.float32)],
        input_output_aliases={1: 0},
        compiler_params=pltpu.CompilerParams(vmem_limit_bytes=20 << 20),
        name="middle",
    )(ints, begun, *panels)


def finish(ints, nearly, panels):
    blocks, size, _ = panels[0].shape
    ordered = jax.ShapeDtypeStruct(nearly.shape, panels[0].dtype)
    return pl.pallas_call(
        last_kernel,
        out_shape=[ordered, jax.ShapeDtypeStruct(nearly.shape, nearly.dtype)],
        in_specs=[SMEM] + [VMEM] * (1 + len(panels)),
        out_specs=[FAR, VMEM],
        scratch_shapes=[
            pltpu.VMEM((blocks * blocks, size, size), jnp.float32),
            pltpu.VMEM(ordered.shape, ordered.dtype),
            pltpu.SemaphoreType.DMA((SLOTS // 4,)),
        ],
        input_output_aliases={1: 1},
        compiler_params=pltpu.CompilerParams(vmem_limit_bytes=20 << 20),
        name="finish",
    )(ints, nearly, *panels)[0]


def body(a_panels, b_panels, pair_lists, pair_counts, keep_mask, send_order, recv_order):
    a0 = a_panels[0, 0]
    b0 = b_panels[0, 0]
    row = lax.axis_index("row").astype(jnp.int32)
    ints = jnp.concatenate([
        lax.rem(row, RUN).reshape(1), pair_counts.reshape(-1), pair_lists.reshape(-1),
        keep_mask.reshape(-1), send_order.reshape(-1),
    ])
    cross = shift(b0, "row", 3)
    near1 = row_hop(b0, 1, (0, 1, 2))
    a1, a2, a3 = (shift(a0, "col", by) for by in (1, 2, 3))
    rows = lax.axis_size("row")
    fellow = lax.all_gather(
        b0, "row", axis_index_groups=[[i, i + 2] for i in range(rows) if i % RUN < 2]
    )
    cross, near1, fellow, ints = lax.optimization_barrier((cross, near1, fellow, ints))
    far2 = row_hop(cross, -1, (2, 3))
    far1 = row_hop(cross, -2, (3,))
    begun = begin(ints, a0, fellow)
    nearly = middle(ints, begun, (a1, a2, a3, near1, fellow, cross))
    ordered = finish(ints, nearly, (a1, a2, far1, far2))
    received = lax.all_to_all(ordered, "col", split_axis=0, concat_axis=0, tiled=True)
    return received[recv_order[0, 0]][None, None]


def solution(mesh):
    return jax.shard_map(
        body,
        mesh=mesh,
        in_specs=(
            P("row", "col", None, None, None),
            P("row", "col", None, None, None),
            P("row", "col", None, None, None),
            P("row", "col", None),
            P("row", "col", None),
            P("row", "col", None),
            P("row", "col", None),
        ),
        out_specs=P("row", "col", None, None, None),
        check_vma=False,
    )
```
